256 devices in a mesh: ctx: 32 (over y, x, core), head: 8 (over z).
Axes of the slice: x: 4, y: 4, z: 8, core: 2. Of those that a mesh axis runs over, the one named last changes fastest.
Arguments:
- queries: bfloat16 [8192, 4096], P('ctx', 'head'), may hold values from -6 to 6
- keys: bfloat16 [8192, 4096], P('ctx', 'head'), may hold values from -6 to 6
- values: bfloat16 [8192, 4096], P('ctx', 'head'), may hold values from -6 to 6
- doc_ids: int32 [8192], P('ctx'), may hold values from 0 to 3, never falling along the last dimension, each value on 1 to 4096 neighbouring positions
- w_out: bfloat16 [4096, 8192], P('head'), may hold values from -0.09375 to 0.09375
Outputs:
- mixed: bfloat16 [8192, 8192], P(('ctx', 'head'))
The draws below stay inside these ranges and needn't reach their ends.
Inputs may be any that keep to these rules, and one draw needn't show every extreme that they name: `doc_ids`: never falls along the sequence; each of the 4 documents holds 1 to 4096 consecutive tokens, and one holds exactly 4096.
All inputs are finite; a program needn't handle non-finite values.
Results may differ from the reference program's by a relative error of at most 0.022.
Values may be sent and summed in bfloat16 or wider, within the bound.
No kernel may reach another device: no remote copies, remote signals or barrier semaphores. Data moves between devices by JAX's collectives and lax.ppermute only.
A program may use at most 128 MiB of HBM per device.

```python
import math
import jax
import jax.numpy as jnp
import numpy as np
from jax import lax

D = 8192
HEADS = 32
DH = 128
SPAN = 256
ITERS = 10
DOCS = 4
TOK_DEV = 256
LENGTH = 8192
N_HEAD = 8


def block_scale(own_key, dims, split, low, largest):
    level, own = 1.0, jax.random.fold_in(own_key, 6)
    for dim, shards_of in split:
        draws = jnp.exp(jax.random.uniform(jax.random.fold_in(own, dim), (shards_of,), jnp.float32, low / len(split), largest / len(split)))
        level = level * jnp.repeat(draws, dims[dim] // shards_of).reshape([-1 if axis == dim else 1 for axis in range(len(dims))])
    return level


def split_up(count, total, reach, slope):
    portions = [(1 << 20) // math.isqrt(grade ** slope) + 1 for grade in range(2, count + 1)]
    surplus, given = total - reach - (count - 1), [1] * (count - 1)
    while surplus > 0:
        candidates = [i for i in range(count - 1) if given[i] < reach]
        mass, budget = sum([portions[i] for i in candidates]), surplus
        for i in candidates:
            extra = min(reach - given[i], max(1, budget * portions[i] // mass), surplus)
            given[i] = given[i] + extra
            surplus = surplus - extra
    return np.array([reach] + given)


def ragged(own_key, number_of, total, limit, slope):
    if number_of == 2:
        one = jax.random.randint(own_key, (), max(1, total - limit), min(limit, total - 1) + 1)
        return jnp.stack([one, total - one])
    tallies = jnp.asarray(split_up(number_of, total, limit, slope), jnp.int32)
    pairs = (number_of - 1) // 2
    giver, sink = tallies[1:1 + 2 * pairs:2], tallies[2:2 + 2 * pairs:2]
    margin = jnp.minimum(giver - 1, limit - sink)
    moved = jax.random.randint(jax.random.fold_in(own_key, 1), (pairs,), 0, 1 << 20) % (margin + 1)
    tallies = tallies.at[1:1 + 2 * pairs:2].set(giver - moved).at[2:2 + 2 * pairs:2].set(sink + moved)
    return tallies[jax.random.permutation(jax.random.fold_in(own_key, 2), number_of)]


def bell_draw(rng, shape, scale, limit, shards=(), dtype=jnp.bfloat16):
    values = jax.random.normal(rng, shape, jnp.float32) * scale
    if len(shards) > 0:
        values = block_scale(rng, shape, shards, -0.22, 0.18) * values
    return jnp.clip(values, min=-limit, max=limit).astype(dtype)


def setup_inputs(seed: int = 0) -> dict:
    arg_keys = jax.random.split(jax.random.key(seed), 6)
    queries = bell_draw(arg_keys[0], (LENGTH, HEADS * DH), 1.0, 6.0, ((0, 32), (1, 8)))
    keys = bell_draw(arg_keys[1], (LENGTH, HEADS * DH), 1.0, 6.0, ((0, 32), (1, 8)))
    values = bell_draw(arg_keys[2], (LENGTH, HEADS * DH), 1.0, 6.0, ((0, 32), (1, 8)))
    doc_ids = jnp.searchsorted(jnp.cumsum(ragged(arg_keys[3], DOCS, LENGTH, LENGTH // 2, 0)), jnp.arange(LENGTH), side="right").astype(jnp.int32)
    w_out = bell_draw(arg_keys[4], (HEADS * DH, D), (HEADS * DH) ** -0.5, 0.09375, ((0, 8),))
    return {"queries": queries, "keys": keys, "values": values, "doc_ids": doc_ids, "w_out": w_out}


ridge_lambda = 0.02
upper_end = 1.0 + ridge_lambda
center = (upper_end + ridge_lambda) / 2.0
radius = (upper_end - ridge_lambda) / 2.0
highest = lax.Precision.HIGHEST

def normalize(block):
    return block * lax.rsqrt(lax.optimization_barrier(jnp.mean(block * block, axis=-1, keepdims=True)) + 1e-06) * (1.0 / math.sqrt(block.shape[-1]))

def one_head(inputs):
    query, key_rows, value_rows, segment = inputs
    query_n = normalize(query)
    key_n = normalize(key_rows)
    nblocks = query.shape[0] // SPAN
    query_c = query_n.reshape(nblocks, SPAN, DH)
    key_c = key_n.reshape(nblocks, SPAN, DH)
    value_c = value_rows.reshape(nblocks, SPAN, DH)
    seg_c = segment.reshape(nblocks, SPAN)

    def advance(carry, blocks):
        state_k, state_v, state_n, last_id = carry
        key_b, value_b, seg_b = blocks
        keep = seg_b[-1] == last_id
        member = (seg_b == seg_b[-1]).astype(jnp.float32)
        new_k = jnp.where(keep, state_k, 0.0) + jnp.einsum('td,te->de', key_b * member[:, None], key_b, precision=highest)
        new_v = jnp.where(keep, state_v, 0.0) + jnp.einsum('td,te->de', value_b * member[:, None], key_b, precision=highest)
        new_n = jnp.where(keep, state_n, 0.0) + jnp.sum(member)
        return ((new_k, new_v, new_n, seg_b[-1]), (state_k, state_v, state_n, last_id))
    start = (jnp.zeros((DH, DH), jnp.float32), jnp.zeros((DH, DH), jnp.float32), jnp.zeros((), jnp.float32), -jnp.ones((), jnp.float32))
    _, (prior_k, prior_v, prior_n, prior_last) = lax.scan(advance, start, (key_c, value_c, seg_c))
    prior_mask = (seg_c == prior_last[:, None]).astype(jnp.float32)
    positions = jnp.arange(SPAN)
    causal = positions[None, :] <= positions[:, None]
    inside = (causal[None] & (seg_c[:, :, None] == seg_c[:, None, :])).astype(jnp.float32)
    counts = prior_mask * prior_n[:, None] + lax.optimization_barrier(jnp.sum(inside, axis=-1))
    inverse = 1.0 / counts

    def scores(field):
        return jnp.einsum('ctd,csd->cts', field, key_c, precision=highest) * inside

    def apply(field):
        before = jnp.einsum('cde,cte->ctd', prior_k, field, precision=highest) * prior_mask[:, :, None]
        within = jnp.einsum('cts,csd->ctd', scores(field), key_c, precision=highest)
        return (before + within) * inverse[:, :, None] + ridge_lambda * field

    def turn(step, state):
        iterate, remain, search, factor = state
        iterate = iterate + search
        remain = remain - apply(search)
        factor_new = 1.0 / (2.0 * center / radius - factor)
        search = factor_new * factor * search + 2.0 * factor_new / radius * remain
        return (iterate, remain, search, factor_new)
    state = (jnp.zeros_like(query_c), query_c, query_c / center, jnp.asarray(radius / center, jnp.float32))
    iterate, remain, search, factor = lax.fori_loop(0, ITERS, turn, state)
    iterate = iterate + search
    output = jnp.einsum('cde,cte->ctd', prior_v, iterate, precision=highest) * prior_mask[:, :, None]
    output = output + jnp.einsum('cts,csd->ctd', scores(iterate), value_c, precision=highest)
    output = normalize(output) * math.sqrt(DH)
    return output.reshape(nblocks * SPAN, DH)

def reference(queries, keys, values, doc_ids, w_out):

    def per_head(array):
        return array.astype(jnp.float32).reshape(LENGTH, HEADS, DH).transpose(1, 0, 2)
    segment = doc_ids.astype(jnp.float32)
    segments = jnp.broadcast_to(segment[None], (HEADS, LENGTH))
    heads_out = lax.map(one_head, (per_head(queries), per_head(keys), per_head(values), segments))
    mixed_in = heads_out.transpose(1, 0, 2).reshape(LENGTH, HEADS * DH).astype(jnp.bfloat16)
    group = HEADS * DH // N_HEAD

    def block_out(rows_block):
        total = jnp.zeros((rows_block.shape[0], D), jnp.float32)
        for index in range(N_HEAD):
            part = jnp.dot(rows_block[:, index * group:(index + 1) * group], w_out[index * group:(index + 1) * group], preferred_element_type=jnp.float32).astype(jnp.bfloat16)
            total = total + lax.optimization_barrier(part).astype(jnp.float32)
        return total.astype(jnp.bfloat16)
    blocks = mixed_in.reshape(LENGTH // TOK_DEV, TOK_DEV, HEADS * DH)
    return lax.map(block_out, blocks).reshape(LENGTH, D)
```

```python
import functools
import math

import jax
import jax.numpy as jnp
from jax import lax
from jax.experimental import pallas as pl
from jax.experimental.pallas import tpu as pltpu
from jax.sharding import PartitionSpec as P

DH = 128
ITERS = 10
N_HEAD = 8

ridge_lambda = 0.02
upper_end = 1.0 + ridge_lambda
center = (upper_end + ridge_lambda) / 2.0
radius = (upper_end - ridge_lambda) / 2.0

f32 = jnp.float32
bf16 = jnp.bfloat16


def dot(a, b):
    return jnp.dot(a, b, preferred_element_type=f32)


def split(field):
    high = field.astype(bf16)
    low = (field - high.astype(f32)).astype(bf16)
    return jnp.concatenate([high, low], axis=1)


def scale_of(rows):
    return lax.rsqrt(jnp.mean(rows * rows, axis=-1, keepdims=True) + 1e-06) * (
        1.0 / math.sqrt(DH)
    )


def tails_kernel(k_ref, v_ref, doc_ref, send_ref, kt_ref):
    tokens, width = k_ref.shape
    heads = width // DH
    doc = doc_ref[...].astype(f32)
    last = jnp.max(doc)
    member_row = (doc == last).astype(f32)
    member = jnp.broadcast_to(member_row, (DH, tokens)).T
    parts = send_ref.shape[0]
    size = send_ref.shape[1] - 16
    per = DH // size
    for h in range(heads):
        cols = slice(h * DH, (h + 1) * DH)
        k = k_ref[:, cols].astype(f32)
        scale = scale_of(k) * member
        kt = k.T.astype(bf16)
        kt_ref[h * DH : (h + 1) * DH, :] = kt
        right = jnp.concatenate(
            [k * (scale * scale), v_ref[:, cols].astype(f32) * scale], axis=1
        ).astype(bf16)
        state = dot(kt, right).astype(bf16)
        send_ref[h * per : (h + 1) * per, :size, :] = state[:, :DH].reshape(per, size, DH)
        base = (heads + h) * per
        send_ref[base : base + per, :size, :] = state[:, DH:].reshape(per, size, DH)
    number = jnp.broadcast_to(jnp.sum(member_row, axis=1, keepdims=True), (8, DH))
    note = jnp.concatenate([jnp.full((8, DH), last), number], axis=0).astype(bf16)
    send_ref[:, size:, :] = jnp.broadcast_to(note[None], (parts, 16, DH))


def prefix_kernel(recv_ref, send_ref, meta_ref):
    blocks, rows, _ = recv_ref.shape
    size = rows - 16
    me = lax.axis_index("ctx")
    state = jnp.zeros((size, DH), f32)
    number = jnp.zeros((8, DH), f32)
    last = jnp.full((8, DH), -1.0, f32)
    mine_number, mine_last = number, last
    for b in range(blocks):
        mine_number = jnp.where(me == b, number, mine_number)
        mine_last = jnp.where(me == b, last, mine_last)
        send_ref[b] = state.astype(bf16)
        note = recv_ref[b, size:, :].astype(f32)
        keep = (note[:8] == last).astype(f32)
        state = state * keep[:1] + recv_ref[b, :size, :].astype(f32)
        number = number * keep + note[8:]
        last = note[:8]
    meta_ref[:8] = mine_number
    meta_ref[8:] = mine_last


def solve_kernel(
    offsets,
    pieces,
    q_ref,
    k_ref,
    v_ref,
    doc_ref,
    kt_ref,
    state_ref,
    meta_ref,
    w_ref,
    *rest,
):
    outs = rest[: len(pieces)]
    w_vmem, doc_col, right, weight, p_ref, r_ref, x_ref, w_sem = rest[len(pieces) :]
    tokens, width = q_ref.shape
    heads = width // DH
    share = tokens // N_HEAD
    load = pltpu.make_async_copy(w_ref, w_vmem, w_sem)
    load.start()
    me = lax.axis_index("head")
    starts = [pl.multiple_of(lax.rem(me + o, N_HEAD) * share, share) for o in offsets]
    rows = share * len(offsets)

    doc = doc_ref[...].astype(f32)
    doc_col[...] = jnp.broadcast_to(doc, (DH, tokens)).T
    mine = jnp.concatenate([doc_col[pl.ds(s, share), :] for s in starts], axis=0)
    inner = lax.broadcasted_iota(jnp.int32, (share, tokens), 0)
    when = jnp.concatenate([inner + s for s in starts], axis=0)
    position = lax.broadcasted_iota(jnp.int32, (rows, tokens), 1)
    wide = jnp.concatenate([mine, mine], axis=1)
    inside = ((position <= when) & (wide == doc)).astype(f32)
    prior = (mine == meta_ref[8:9, :]).astype(f32)
    counts = prior * meta_ref[0:1, :] + jnp.sum(inside, axis=1, keepdims=True)
    inverse = 1.0 / counts
    prior_inverse = prior * inverse
    inside_inverse = inside * jnp.concatenate([inverse, inverse], axis=1)
    ones = jnp.ones((8, DH), f32)

    for h in range(heads):
        cols = slice(h * DH, (h + 1) * DH)
        kt = kt_ref[cols, :]
        ktf = kt.astype(f32)
        mean = jnp.mean(ktf * ktf, axis=0, keepdims=True)
        scale = lax.rsqrt(mean + 1e-06) * (1.0 / math.sqrt(DH))
        weight[h] = inside_inverse * (scale * scale)
        state = state_ref[cols, :]
        right[h, :DH, :tokens] = kt
        right[h, DH:, :tokens] = kt
        right[h, :DH, tokens:] = state
        right[h, DH:, tokens:] = state
        q = jnp.concatenate([q_ref[pl.ds(s, share), cols] for s in starts], axis=0).astype(f32)
        q = q * scale_of(q)
        r_ref[h] = q
        p_ref[h] = q * (1.0 / center)
        x_ref[h] = q * (1.0 / center)

    factor = radius / center
    for _ in range(ITERS):
        factor_new = 1.0 / (2.0 * center / radius - factor)
        for h in range(heads):
            p = p_ref[h]
            both = dot(split(p), right[h])
            scores = (both[:, :tokens] * weight[h]).astype(bf16)
            moved = dot(scores, k_ref[:, h * DH : (h + 1) * DH])
            r = r_ref[h] - (moved + both[:, tokens:] * prior_inverse + ridge_lambda * p)
            p = (factor_new * factor) * p + (2.0 * factor_new / radius) * r
            r_ref[h] = r
            p_ref[h] = p
            x_ref[h] = x_ref[h] + p
        factor = factor_new

    ys = []
    for h in range(heads):
        cols = slice(h * DH, (h + 1) * DH)
        ktf = kt_ref[cols, :].astype(f32)
        mean = jnp.mean(ktf * ktf, axis=0, keepdims=True)
        scale = lax.rsqrt(mean + 1e-06) * (1.0 / math.sqrt(DH))
        state = state_ref[width + h * DH : width + (h + 1) * DH, :]
        right[h, :DH, tokens:] = state
        right[h, DH:, tokens:] = state
        both = dot(split(x_ref[h]), right[h])
        scores = (both[:, :tokens] * (inside * scale)).astype(bf16)
        o = dot(scores, v_ref[:, cols]) + both[:, tokens:] * prior
        o = o * lax.rsqrt(jnp.mean(o * o, axis=-1, keepdims=True) + 1e-06)
        ys.append(o.astype(bf16))
    y = jnp.concatenate(ys, axis=1)
    load.wait()
    model = w_vmem.shape[1]
    tile = 1024
    for c in range(0, model, tile):
        part = dot(y, w_vmem[:, c : c + tile]).astype(bf16)
        for out, (at, lo, hi) in zip(outs, pieces):
            if lo <= c < hi:
                out[:, c - lo : c - lo + tile] = part[at * share : (at + 1) * share]


def solve(offsets, pieces, q, k, v, doc, kt, state, meta, w):
    tokens, width = q.shape
    heads = width // DH
    share = tokens // N_HEAD
    rows = share * len(offsets)
    vmem = pl.BlockSpec(memory_space=pltpu.VMEM)
    return pl.pallas_call(
        functools.partial(solve_kernel, offsets, pieces),
        out_shape=[jax.ShapeDtypeStruct((share, hi - lo), bf16) for _, lo, hi in pieces],
        in_specs=[vmem] * 7 + [pl.BlockSpec(memory_space=pl.ANY)],
        out_specs=[vmem] * len(pieces),
        scratch_shapes=[
            pltpu.VMEM(w.shape, bf16),
            pltpu.VMEM((tokens, DH), f32),
            pltpu.VMEM((heads, 2 * DH, tokens + DH), bf16),
            pltpu.VMEM((heads, rows, tokens), f32),
            pltpu.VMEM((heads, rows, DH), f32),
            pltpu.VMEM((heads, rows, DH), f32),
            pltpu.VMEM((heads, rows, DH), f32),
            pltpu.SemaphoreType.DMA,
        ],
        compiler_params=pltpu.CompilerParams(vmem_limit_bytes=40 << 20),
        cost_estimate=pl.CostEstimate(
            flops=rows * 50_000_000, bytes_accessed=12_000_000, transcendentals=0
        ),
    )(q, k, v, doc, kt, state, meta, w)


def shards(queries, keys, values, doc_ids, w_out):
    tokens, width = queries.shape
    heads = width // DH
    model = w_out.shape[1]
    half = model // 2
    share = tokens // N_HEAD
    blocks = lax.axis_size("ctx")
    doc = doc_ids.reshape(1, tokens)
    vmem = pl.BlockSpec(memory_space=pltpu.VMEM)
    size = 2 * heads * DH // blocks
    with jax.named_scope("tails"):
        send, kt = pl.pallas_call(
            tails_kernel,
            out_shape=[
                jax.ShapeDtypeStruct((blocks, size + 16, DH), bf16),
                jax.ShapeDtypeStruct((width, tokens), bf16),
            ],
            in_specs=[vmem] * 3,
            out_specs=[vmem] * 2,
        )(keys, values, doc)
    with jax.named_scope("collect"):
        recv = lax.all_to_all(send, "ctx", 0, 0, tiled=True)
    with jax.named_scope("prefix"):
        back, meta = pl.pallas_call(
            prefix_kernel,
            out_shape=[
                jax.ShapeDtypeStruct((blocks, size, DH), bf16),
                jax.ShapeDtypeStruct((16, DH), f32),
            ],
            in_specs=[vmem],
            out_specs=[vmem] * 2,
        )(recv)
    with jax.named_scope("distribute"):
        state = lax.all_to_all(back, "ctx", 0, 0, tiled=True).reshape(2 * width, DH)

    def run(offsets):
        pieces = []
        for at in range(len(offsets)):
            pieces += [(at, 0, half), (at, half, model)]
        got = solve(
            offsets, tuple(pieces), queries, keys, values, doc, kt, state, meta, w_out
        )
        return {(o, c): got[2 * at + c] for at, o in enumerate(offsets) for c in range(2)}

    size_ring = lax.axis_size("head")

    def hop(x, step):
        return lax.ppermute(x, "head", [(i, (i + step) % size_ring) for i in range(size_ring)])

    with jax.named_scope("far_tokens"):
        part = run((4, 3, 5))
    with jax.named_scope("near_tokens"):
        part.update(run((2, 6, 1, 7, 0)))

    def add(a, b):
        return (a.astype(f32) + b.astype(f32)).astype(bf16)

    sums = []
    for step, first in ((1, 0), (-1, 1)):
        second = 1 - first
        with jax.named_scope("ring"):
            a = hop(part[4, first], step)
            b = hop(part[(3 * step) % 8, second], step)
            a = hop(add(a, part[(3 * step) % 8, first]), step)
            for distance in (2, 1):
                b = hop(add(b, part[(distance * step) % 8, second]), step)
                a = hop(add(a, part[(distance * step) % 8, first]), step)
        sums.append({first: a, second: b})
    columns = [
        (
            sums[0][c].astype(f32) + sums[1][c].astype(f32) + part[0, c].astype(f32)
        ).astype(bf16)
        for c in range(2)
    ]
    return jnp.concatenate(columns, axis=1)


def solution(mesh):
    return jax.shard_map(
        shards,
        mesh=mesh,
        in_specs=(P("ctx", "head"), P("ctx", "head"), P("ctx", "head"), P("ctx"), P("head", None)),
        out_specs=P(("ctx", "head"), None),
        check_vma=False,
    )
```

```python
import functools
import math

import jax
import jax.numpy as jnp
from jax import lax
from jax.experimental import pallas as pl
from jax.experimental.pallas import tpu as pltpu
from jax.sharding import PartitionSpec as P

DH = 128
ITERS = 10
N_HEAD = 8
STREAMS = ((1, 0, "a"), (-1, 1, "a"), (-1, 0, "b"), (1, 1, "b"))
LIMIT = 50
FAR = (4, 3, 5, 2, 6, 1, 7, 0)
NEAR = ()

ridge_lambda = 0.02
upper_end = 1.0 + ridge_lambda
center = (upper_end + ridge_lambda) / 2.0
radius = (upper_end - ridge_lambda) / 2.0

f32 = jnp.float32
bf16 = jnp.bfloat16


def dot(a, b):
    return jnp.dot(a, b, preferred_element_type=f32)


def split(field):
    high = field.astype(bf16)
    low = (field - high.astype(f32)).astype(bf16)
    return jnp.concatenate([high, low], axis=1)


def scale_of(rows):
    return lax.rsqrt(jnp.mean(rows * rows, axis=-1, keepdims=True) + 1e-06) * (
        1.0 / math.sqrt(DH)
    )


def tails_kernel(k_ref, v_ref, doc_ref, send_ref, kt_ref):
    tokens, width = k_ref.shape
    heads = width // DH
    doc = doc_ref[...].astype(f32)
    last = jnp.max(doc)
    member_row = (doc == last).astype(f32)
    member = jnp.broadcast_to(member_row, (DH, tokens)).T
    parts = send_ref.shape[0]
    size = send_ref.shape[1] - 16
    per = DH // size
    for h in range(heads):
        cols = slice(h * DH, (h + 1) * DH)
        k = k_ref[:, cols].astype(f32)
        scale = scale_of(k) * member
        kt = k.T.astype(bf16)
        kt_ref[h * DH : (h + 1) * DH, :] = kt
        right = jnp.concatenate(
            [k * (scale * scale), v_ref[:, cols].astype(f32) * scale], axis=1
        ).astype(bf16)
        state = dot(kt, right).astype(bf16)
        send_ref[h * per : (h + 1) * per, :size, :] = state[:, :DH].reshape(per, size, DH)
        base = (heads + h) * per
        send_ref[base : base + per, :size, :] = state[:, DH:].reshape(per, size, DH)
    number = jnp.broadcast_to(jnp.sum(member_row, axis=1, keepdims=True), (8, DH))
    note = jnp.concatenate([jnp.full((8, DH), last), number], axis=0).astype(bf16)
    send_ref[:, size:, :] = jnp.broadcast_to(note[None], (parts, 16, DH))


def prefix_kernel(recv_ref, send_ref, meta_ref):
    blocks, rows, _ = recv_ref.shape
    size = rows - 16
    me = lax.axis_index("ctx")
    state = jnp.zeros((size, DH), f32)
    number = jnp.zeros((8, DH), f32)
    last = jnp.full((8, DH), -1.0, f32)
    mine_number, mine_last = number, last
    for b in range(blocks):
        mine_number = jnp.where(me == b, number, mine_number)
        mine_last = jnp.where(me == b, last, mine_last)
        send_ref[b] = state.astype(bf16)
        note = recv_ref[b, size:, :].astype(f32)
        keep = (note[:8] == last).astype(f32)
        state = state * keep[:1] + recv_ref[b, :size, :].astype(f32)
        number = number * keep + note[8:]
        last = note[:8]
    meta_ref[:8] = mine_number
    meta_ref[8:] = mine_last


def solve_kernel(offsets, pieces, *refs):
    hbm, refs = refs[:8], refs[8:]
    outs, refs = refs[: len(pieces)], refs[len(pieces) :]
    held, (doc_col, right, weight, p_ref, r_ref, x_ref, sems) = refs[:8], refs[8:]
    loads = [pltpu.make_async_copy(a, b, sems.at[i]) for i, (a, b) in enumerate(zip(hbm, held))]
    for load in loads:
        load.start()
    q_ref, k_ref, v_ref, doc_ref, kt_ref, state_ref, meta_ref, w_vmem = held
    tokens, width = q_ref.shape
    heads = width // DH
    share = tokens // N_HEAD
    for load in loads[:-1]:
        load.wait()
    me = lax.axis_index("head")
    starts = [pl.multiple_of(lax.rem(me + o, N_HEAD) * share, share) for o in offsets]
    rows = share * len(offsets)

    doc = doc_ref[...].astype(f32)
    doc_col[...] = jnp.broadcast_to(doc, (DH, tokens)).T
    mine = jnp.concatenate([doc_col[pl.ds(s, share), :] for s in starts], axis=0)
    inner = lax.broadcasted_iota(jnp.int32, (share, tokens), 0)
    when = jnp.concatenate([inner + s for s in starts], axis=0)
    position = lax.broadcasted_iota(jnp.int32, (rows, tokens), 1)
    wide = jnp.concatenate([mine, mine], axis=1)
    inside = ((position <= when) & (wide == doc)).astype(f32)
    prior = (mine == meta_ref[8:9, :]).astype(f32)
    counts = prior * meta_ref[0:1, :] + jnp.sum(inside, axis=1, keepdims=True)
    inverse = 1.0 / counts
    prior_inverse = prior * inverse
    inside_inverse = inside * jnp.concatenate([inverse, inverse], axis=1)
    ones = jnp.ones((8, DH), f32)

    for h in range(heads):
        cols = slice(h * DH, (h + 1) * DH)
        kt = kt_ref[cols, :]
        ktf = kt.astype(f32)
        mean = jnp.mean(ktf * ktf, axis=0, keepdims=True)
        scale = lax.rsqrt(mean + 1e-06) * (1.0 / math.sqrt(DH))
        weight[h] = inside_inverse * (scale * scale)
        state = state_ref[cols, :]
        right[h, :DH, :tokens] = kt
        right[h, DH:, :tokens] = kt
        right[h, :DH, tokens:] = state
        right[h, DH:, tokens:] = state
        q = jnp.concatenate([q_ref[pl.ds(s, share), cols] for s in starts], axis=0).astype(f32)
        q = q * scale_of(q)
        r_ref[h] = q
        p_ref[h] = q * (1.0 / center)
        x_ref[h] = q * (1.0 / center)

    factor = radius / center
    for _ in range(ITERS):
        factor_new = 1.0 / (2.0 * center / radius - factor)
        for h in range(heads):
            p = p_ref[h]
            both = dot(split(p), right[h])
            scores = (both[:, :tokens] * weight[h]).astype(bf16)
            moved = dot(scores, k_ref[:, h * DH : (h + 1) * DH])
            r = r_ref[h] - (moved + both[:, tokens:] * prior_inverse + ridge_lambda * p)
            p = (factor_new * factor) * p + (2.0 * factor_new / radius) * r
            r_ref[h] = r
            p_ref[h] = p
            x_ref[h] = x_ref[h] + p
        factor = factor_new

    ys = []
    for h in range(heads):
        cols = slice(h * DH, (h + 1) * DH)
        ktf = kt_ref[cols, :].astype(f32)
        mean = jnp.mean(ktf * ktf, axis=0, keepdims=True)
        scale = lax.rsqrt(mean + 1e-06) * (1.0 / math.sqrt(DH))
        state = state_ref[width + h * DH : width + (h + 1) * DH, :]
        right[h, :DH, tokens:] = state
        right[h, DH:, tokens:] = state
        both = dot(split(x_ref[h]), right[h])
        scores = (both[:, :tokens] * (inside * scale)).astype(bf16)
        o = dot(scores, v_ref[:, cols]) + both[:, tokens:] * prior
        o = o * lax.rsqrt(jnp.mean(o * o, axis=-1, keepdims=True) + 1e-06)
        ys.append(o.astype(bf16))
    y = jnp.concatenate(ys, axis=1)
    loads[-1].wait()
    model = w_vmem.shape[1]
    tile = 1024
    for c in range(0, model, tile):
        part = dot(y, w_vmem[:, c : c + tile]).astype(bf16)
        for out, (at, lo, hi) in zip(outs, pieces):
            if lo <= c < hi:
                out[:, c - lo : c - lo + tile] = part[at * share : (at + 1) * share]


def solve(offsets, pieces, q, k, v, doc, kt, state, meta, w):
    tokens, width = q.shape
    heads = width // DH
    share = tokens // N_HEAD
    rows = share * len(offsets)
    vmem = pl.BlockSpec(memory_space=pltpu.VMEM)
    args = (q, k, v, doc, kt, state, meta, w)
    return pl.pallas_call(
        functools.partial(solve_kernel, offsets, pieces),
        out_shape=[jax.ShapeDtypeStruct((share, hi - lo), bf16) for _, lo, hi in pieces],
        in_specs=[pl.BlockSpec(memory_space=pltpu.HBM)] * len(args),
        out_specs=[vmem] * len(pieces),
        scratch_shapes=[
            *[pltpu.VMEM(a.shape, a.dtype) for a in args],
            pltpu.VMEM((tokens, DH), f32),
            pltpu.VMEM((heads, 2 * DH, tokens + DH), bf16),
            pltpu.VMEM((heads, rows, tokens), f32),
            pltpu.VMEM((heads, rows, DH), f32),
            pltpu.VMEM((heads, rows, DH), f32),
            pltpu.VMEM((heads, rows, DH), f32),
            pltpu.SemaphoreType.DMA((len(args),)),
        ],
        compiler_params=pltpu.CompilerParams(vmem_limit_bytes=LIMIT << 20),
        cost_estimate=pl.CostEstimate(
            flops=rows * 50_000_000, bytes_accessed=12_000_000, transcendentals=0
        ),
    )(*args)


def shards(queries, keys, values, doc_ids, w_out):
    tokens, width = queries.shape
    heads = width // DH
    model = w_out.shape[1]
    half = model // 2
    share = tokens // N_HEAD
    blocks = lax.axis_size("ctx")
    doc = doc_ids.reshape(1, tokens)
    vmem = pl.BlockSpec(memory_space=pltpu.VMEM)
    size = 2 * heads * DH // blocks
    with jax.named_scope("tails"):
        send, kt = pl.pallas_call(
            tails_kernel,
            out_shape=[
                jax.ShapeDtypeStruct((blocks, size + 16, DH), bf16),
                jax.ShapeDtypeStruct((width, tokens), bf16),
            ],
            in_specs=[vmem] * 3,
            out_specs=[vmem] * 2,
        )(keys, values, doc)
    with jax.named_scope("collect"):
        recv = lax.all_to_all(send, "ctx", 0, 0, tiled=True)
    with jax.named_scope("prefix"):
        back, meta = pl.pallas_call(
            prefix_kernel,
            out_shape=[
                jax.ShapeDtypeStruct((blocks, size, DH), bf16),
                jax.ShapeDtypeStruct((16, DH), f32),
            ],
            in_specs=[vmem],
            out_specs=[vmem] * 2,
        )(recv)
    with jax.named_scope("distribute"):
        state = lax.all_to_all(back, "ctx", 0, 0, tiled=True).reshape(2 * width, DH)

    def run(offsets, meta):
        pieces = []
        for at in range(len(offsets)):
            pieces += [(at, 0, half), (at, half, model)]
        got = solve(
            offsets, tuple(pieces), queries, keys, values, doc, kt, state, meta, w_out
        )
        return {(o, c): got[2 * at + c] for at, o in enumerate(offsets) for c in range(2)}

    size_ring = lax.axis_size("head")

    def hop(x, step):
        return lax.ppermute(x, "head", [(i, (i + step) % size_ring) for i in range(size_ring)])

    latest = None

    def add(a, b):
        nonlocal latest
        if latest is not None:
            b, _ = lax.optimization_barrier((b, latest))
        latest = (a.astype(f32) + b.astype(f32)).astype(bf16)
        return latest

    with jax.named_scope("far_tokens"):
        part = run(FAR, meta)
    moving = {}
    with jax.named_scope("ring"):
        for step, c, kind in STREAMS:
            first = 4 if kind == "a" else (3 * step) % N_HEAD
            moving[step, c] = hop(part[first, c], step)
        for turn in range(3):
            for step, c, kind in STREAMS:
                distance = 3 - turn if kind == "a" else 2 - turn
                if distance > 0:
                    latest = None
                    total = add(moving[step, c], part[(distance * step) % N_HEAD, c])
                    moving[step, c] = hop(total, step)
    order = ((1, 0), (-1, 1), (1, 1), (-1, 0))
    moving = dict(zip(order, lax.optimization_barrier(tuple(moving[o] for o in order))))
    sums = [{c: moving[step, c] for c in range(2)} for step in (1, -1)]
    columns = [
        (
            sums[0][c].astype(f32) + sums[1][c].astype(f32) + part[0, c].astype(f32)
        ).astype(bf16)
        for c in range(2)
    ]
    return jnp.concatenate(columns, axis=1)


def solution(mesh):
    return jax.shard_map(
        shards,
        mesh=mesh,
        in_specs=(P("ctx", "head"), P("ctx", "head"), P("ctx", "head"), P("ctx"), P("head", None)),
        out_specs=P(("ctx", "head"), None),
        check_vma=False,
    )
```

```python
import functools
import math

import jax
import jax.numpy as jnp
from jax import lax
from jax.experimental import pallas as pl
from jax.experimental.pallas import tpu as pltpu
from jax.sharding import PartitionSpec as P

DH = 128
ITERS = 10
N_HEAD = 8
CORES = 2
ROW = 4
COLUMN = 4
NOTE = 16
LIMIT = 50
OFFSETS = (4, 3, 5, 2, 6, 1, 7, 0)

ridge_lambda = 0.02
upper_end = 1.0 + ridge_lambda
center = (upper_end + ridge_lambda) / 2.0
radius = (upper_end - ridge_lambda) / 2.0

f32 = jnp.float32
bf16 = jnp.bfloat16


def dot(a, b):
    return jnp.dot(a, b, preferred_element_type=f32)


def split(field):
    high = field.astype(bf16)
    low = (field - high.astype(f32)).astype(bf16)
    return jnp.concatenate([high, low], axis=1)


def scale_of(rows):
    return lax.rsqrt(jnp.mean(rows * rows, axis=-1, keepdims=True) + 1e-06) * (
        1.0 / math.sqrt(DH)
    )


def tails_kernel(k_ref, v_ref, doc_ref, keep_ref, give_ref, kt_ref):
    tokens, width = k_ref.shape
    heads = width // DH
    doc = doc_ref[...].astype(f32)
    last = jnp.max(doc)
    member_row = (doc == last).astype(f32)
    member = jnp.broadcast_to(member_row, (DH, tokens)).T
    first_core = lax.rem(lax.axis_index("ctx"), CORES) == 0
    for h in range(heads):
        cols = slice(h * DH, (h + 1) * DH)
        k = k_ref[:, cols].astype(f32)
        scale = scale_of(k) * member
        kt = k.T.astype(bf16)
        kt_ref[cols, :] = kt
        right = jnp.concatenate(
            [k * (scale * scale), v_ref[:, cols].astype(f32) * scale], axis=1
        ).astype(bf16)
        state = dot(kt, right)
        key_state, value_state = state[:, :DH], state[:, DH:]
        keep_ref[cols, :] = jnp.where(first_core, key_state, value_state).astype(bf16)
        give_ref[cols, :] = jnp.where(first_core, value_state, key_state).astype(bf16)
    kt_ref[width:, :] = jnp.broadcast_to(doc, (NOTE, tokens)).astype(bf16)
    number = jnp.broadcast_to(jnp.sum(member_row, axis=1, keepdims=True), (8, DH))
    sixteens = jnp.floor(number * (1.0 / 16.0))
    note = jnp.concatenate(
        [jnp.full((4, DH), last), sixteens[:4], number - 16.0 * sixteens], axis=0
    ).astype(bf16)
    keep_ref[width:, :] = note
    give_ref[width:, :] = note


def solve_kernel(pieces, *refs):
    hbm, refs = refs[:7], refs[7:]
    outs, refs = refs[: len(pieces)], refs[len(pieces) :]
    held, (right, weight, p_ref, r_ref, x_ref, y_ref, sems) = refs[:7], refs[7:]
    loads = [pltpu.make_async_copy(a, b, sems.at[i]) for i, (a, b) in enumerate(zip(hbm, held))]
    for load in loads:
        load.start()
    q_ref, k_ref, v_ref, kt_ref, mine_ref, back_ref, w_vmem = held
    tokens, width = q_ref.shape
    heads = width // DH
    share = tokens // N_HEAD
    for load in loads[:-1]:
        load.wait()

    first_core = lax.rem(lax.axis_index("ctx"), CORES) == 0
    doc = kt_ref[width : width + NOTE, :].astype(f32)[:1]
    mine = jnp.broadcast_to(doc, (DH, tokens)).T
    note = mine_ref[width : width + NOTE, :].astype(f32)
    causal = lax.broadcasted_iota(jnp.int32, (tokens, tokens), 1) <= lax.broadcasted_iota(
        jnp.int32, (tokens, tokens), 0
    )
    wide = jnp.concatenate([mine] * (tokens // DH), axis=1)
    inside = (causal & (wide == doc)).astype(f32)
    prior = (mine == note[0:1]).astype(f32)
    inverse = 1.0 / (
        prior * (16.0 * note[4:5] + note[8:9]) + jnp.sum(inside, axis=1, keepdims=True)
    )
    prior_inverse = prior * inverse
    inside_inverse = inside * jnp.concatenate([inverse] * (tokens // DH), axis=1)

    scales = []
    for h in range(heads):
        cols = slice(h * DH, (h + 1) * DH)
        kt = kt_ref[cols, :]
        ktf = kt.astype(f32)
        mean = jnp.mean(ktf * ktf, axis=0, keepdims=True)
        scale = lax.rsqrt(mean + 1e-06) * (1.0 / math.sqrt(DH))
        scales.append(scale)
        weight[h] = inside_inverse * (scale * scale)
        state = jnp.where(first_core, mine_ref[cols, :], back_ref[cols, :])
        for at in (0, DH):
            right[h, at : at + DH, :tokens] = kt
            right[h, at : at + DH, tokens:] = state
        q = q_ref[:, cols].astype(f32)
        q = q * scale_of(q)
        r_ref[h] = q
        p_ref[h] = q * (1.0 / center)
        x_ref[h] = q * (1.0 / center)

    def products(field, h, times, rows):
        both = dot(split(field), right[h])
        return dot((both[:, :tokens] * times).astype(bf16), rows), both[:, tokens:]

    factor = radius / center
    for _ in range(ITERS):
        factor_new = 1.0 / (2.0 * center / radius - factor)
        for h in range(heads):
            p = p_ref[h]
            within, far = products(p, h, weight[h], k_ref[:, h * DH : (h + 1) * DH])
            r = r_ref[h] - (within + far * prior_inverse + ridge_lambda * p)
            p = (factor_new * factor) * p + (2.0 * factor_new / radius) * r
            r_ref[h] = r
            p_ref[h] = p
            x_ref[h] = x_ref[h] + p
        factor = factor_new

    for h in range(heads):
        cols = slice(h * DH, (h + 1) * DH)
        scale = scales[h]
        state = jnp.where(first_core, back_ref[cols, :], mine_ref[cols, :])
        for at in (0, DH):
            right[h, at : at + DH, tokens:] = state
        within, far = products(x_ref[h], h, inside * scale, v_ref[:, cols])
        o = within + far * prior
        o = o * lax.rsqrt(jnp.mean(o * o, axis=-1, keepdims=True) + 1e-06)
        y_ref[:, cols] = o.astype(bf16)
    me = lax.axis_index("head")
    y = jnp.concatenate(
        [
            y_ref[pl.ds(pl.multiple_of(lax.rem(me + o, N_HEAD) * share, share), share), :]
            for o in OFFSETS
        ],
        axis=0,
    )
    loads[-1].wait()
    model = w_vmem.shape[1]
    tile = 1024
    for c in range(0, model, tile):
        part = dot(y, w_vmem[:, c : c + tile]).astype(bf16)
        for out, (at, lo, hi) in zip(outs, pieces):
            if lo <= c < hi:
                out[:, c - lo : c - lo + tile] = part[at * share : (at + 1) * share]


def solve(pieces, *args):
    tokens, width = args[0].shape
    heads = width // DH
    share = tokens // N_HEAD
    vmem = pl.BlockSpec(memory_space=pltpu.VMEM)
    return pl.pallas_call(
        functools.partial(solve_kernel, pieces),
        out_shape=[jax.ShapeDtypeStruct((share, hi - lo), bf16) for _, lo, hi in pieces],
        in_specs=[pl.BlockSpec(memory_space=pltpu.HBM)] * len(args),
        out_specs=[vmem] * len(pieces),
        scratch_shapes=[
            *[pltpu.VMEM(a.shape, a.dtype) for a in args],
            pltpu.VMEM((heads, 2 * DH, tokens + DH), bf16),
            pltpu.VMEM((heads, tokens, tokens), f32),
            pltpu.VMEM((heads, tokens, DH), f32),
            pltpu.VMEM((heads, tokens, DH), f32),
            pltpu.VMEM((heads, tokens, DH), f32),
            pltpu.VMEM((tokens, width), bf16),
            pltpu.SemaphoreType.DMA((len(args),)),
        ],
        compiler_params=pltpu.CompilerParams(vmem_limit_bytes=LIMIT << 20),
        cost_estimate=pl.CostEstimate(
            flops=12_000_000_000, bytes_accessed=12_000_000, transcendentals=0
        ),
    )(*args)


def prior_states(keep, give):
    rows = keep.shape[0]
    at = rows - NOTE
    size = lax.axis_size("ctx")
    index = lax.axis_index("ctx")
    core = lax.rem(index, CORES)
    x = lax.rem(index // CORES, ROW)
    y = index // (CORES * ROW)
    counted = lax.broadcasted_iota(jnp.int32, (rows, 1), 0)
    counted = (counted < at) | (counted >= at + 4)

    def across(array):
        return lax.ppermute(array, "ctx", [(i, i ^ 1) for i in range(size)])

    def along_x(array, step):
        def target(i):
            c, xx, yy = i % CORES, i // CORES % ROW, i // (CORES * ROW)
            return (yy * ROW + (xx + step) % ROW) * CORES + c

        return lax.ppermute(array, "ctx", [(i, target(i)) for i in range(size)])

    def along_y(array, step):
        return lax.ppermute(
            array, "ctx", [(i, (i + step * CORES * ROW) % size) for i in range(size)]
        )

    def last(array):
        return array[at : at + 1].astype(f32)

    def gated(array, gate):
        return jnp.where(gate & counted, array.astype(f32), 0.0)

    def named(state, document):
        return jnp.where(counted, state, document).astype(bf16)

    other = across(give)
    early = jnp.where(core == 0, keep, other)
    late = jnp.where(core == 0, other, keep)
    chip = named(
        gated(late, last(late) == last(late)) + gated(early, last(early) == last(late)), last(late)
    )
    one = along_x(chip, 1)
    three = along_x(chip, -1)
    two = along_x(chip, 2)
    row_last = jnp.maximum(
        jnp.maximum(last(one), last(two)), jnp.maximum(last(three), last(chip))
    )
    row = named(
        sum(gated(part, last(part) == row_last) for part in (chip, one, two, three)), row_last
    )
    row_one = along_y(row, 1)
    row_two = along_y(row, 2)
    document = jnp.where(x > 0, last(one), jnp.where(y > 0, last(row_one), -1.0))
    first = sum(
        gated(part, (last(part) == document) & there)
        for part, there in (
            (one, x >= 1),
            (two, x >= 2),
            (three, x >= 3),
            (row_one, y >= 1),
            (row_two, y >= 2),
        )
    )
    second = gated(early, last(early) == last(early)) + jnp.where(
        last(early) == document, first, 0.0
    )
    first = named(first, document)
    second = named(second, last(early))
    mine = jnp.where(core == 0, first, second)
    back = across(jnp.where(core == 0, second, first))
    return mine, back


def shards(queries, keys, values, doc_ids, w_out):
    tokens, width = queries.shape
    model = w_out.shape[1]
    half = model // 2
    doc = doc_ids.reshape(1, tokens)
    vmem = pl.BlockSpec(memory_space=pltpu.VMEM)
    with jax.named_scope("tails"):
        keep, give, kt = pl.pallas_call(
            tails_kernel,
            out_shape=[
                jax.ShapeDtypeStruct((width + NOTE, DH), bf16),
                jax.ShapeDtypeStruct((width + NOTE, DH), bf16),
                jax.ShapeDtypeStruct((width + NOTE, tokens), bf16),
            ],
            in_specs=[vmem] * 3,
            out_specs=[vmem] * 3,
        )(keys, values, doc)
    with jax.named_scope("prior_states"):
        mine, back = prior_states(keep, give)
    pieces = []
    for at in range(N_HEAD):
        pieces += [(at, 0, half), (at, half, model)]
    with jax.named_scope("solve"):
        got = solve(tuple(pieces), queries, keys, values, kt, mine, back, w_out)
    part = {(o, c): got[2 * at + c] for at, o in enumerate(OFFSETS) for c in range(2)}

    size = lax.axis_size("head")

    def hop(array, step):
        return lax.ppermute(array, "head", [(i, (i + step) % size) for i in range(size)])

    def add(*arrays):
        return sum(array.astype(f32) for array in arrays).astype(bf16)

    streams = ((1, 0, 4), (-1, 1, 4), (1, 1, 3), (-1, 0, 3))
    moving = []
    with jax.named_scope("ring"):
        for step, c, hops in streams:
            total = part[hops * step % N_HEAD, c]
            for distance in range(hops - 1, 0, -1):
                total = add(hop(total, step), part[distance * step % N_HEAD, c])
            moving.append(hop(total, step))
    moving = lax.optimization_barrier(tuple(moving))
    columns = [
        add(*[array for array, stream in zip(moving, streams) if stream[1] == c], part[0, c])
        for c in range(2)
    ]
    return jnp.concatenate(columns, axis=1)


def solution(mesh):
    return jax.shard_map(
        shards,
        mesh=mesh,
        in_specs=(P("ctx", "head"), P("ctx", "head"), P("ctx", "head"), P("ctx"), P("head", None)),
        out_specs=P(("ctx", "head"), None),
        check_vma=False,
    )
```

```python
import functools
import math

import jax
import jax.numpy as jnp
from jax import lax
from jax.experimental import pallas as pl
from jax.experimental.pallas import tpu as pltpu
from jax.sharding import PartitionSpec as P

DH = 128
ITERS = 10
N_HEAD = 8
CORES = 2
ROW = 4
COLUMN = 4
NOTE = 16
LIMIT = 198
OFFSETS = (4, 3, 5, 2, 6, 1, 7, 0)

ridge_lambda = 0.02
upper_end = 1.0 + ridge_lambda
center = (upper_end + ridge_lambda) / 2.0
radius = (upper_end - ridge_lambda) / 2.0

f32 = jnp.float32
bf16 = jnp.bfloat16


def dot(a, b):
    return jnp.dot(a, b, preferred_element_type=f32)


def split(field):
    high = field.astype(bf16)
    low = (field - high.astype(f32)).astype(bf16)
    return jnp.concatenate([high, low], axis=1)


def scale_of(rows):
    return lax.rsqrt(jnp.mean(rows * rows, axis=-1, keepdims=True) + 1e-06) * (
        1.0 / math.sqrt(DH)
    )


def tails_kernel(k_ref, v_ref, doc_ref, keep_ref, give_ref, kt_ref):
    tokens, width = k_ref.shape
    heads = width // DH
    doc = doc_ref[...].astype(f32)
    last = jnp.max(doc)
    member_row = (doc == last).astype(f32)
    member = jnp.broadcast_to(member_row, (DH, tokens)).T
    first_core = lax.rem(lax.axis_index("ctx"), CORES) == 0
    for h in range(heads):
        cols = slice(h * DH, (h + 1) * DH)
        k = k_ref[:, cols].astype(f32)
        scale = scale_of(k) * member
        kt = k.T.astype(bf16)
        kt_ref[cols, :] = kt
        right = jnp.concatenate(
            [k * (scale * scale), v_ref[:, cols].astype(f32) * scale], axis=1
        ).astype(bf16)
        state = dot(kt, right)
        key_state, value_state = state[:, :DH], state[:, DH:]
        keep_ref[cols, :] = jnp.where(first_core, key_state, value_state).astype(bf16)
        give_ref[cols, :] = jnp.where(first_core, value_state, key_state).astype(bf16)
    kt_ref[width:, :] = jnp.broadcast_to(doc, (NOTE, tokens)).astype(bf16)
    number = jnp.broadcast_to(jnp.sum(member_row, axis=1, keepdims=True), (8, DH))
    sixteens = jnp.floor(number * (1.0 / 16.0))
    note = jnp.concatenate(
        [jnp.full((4, DH), last), sixteens[:4], number - 16.0 * sixteens], axis=0
    ).astype(bf16)
    keep_ref[width:, :] = note
    give_ref[width:, :] = note


def solve_kernel(pieces, *refs):
    hbm, refs = refs[:7], refs[7:]
    outs, refs = refs[: len(pieces)], refs[len(pieces) :]
    held, (right, weight, p_ref, r_ref, x_ref, y_ref, sems) = refs[:7], refs[7:]
    loads = [pltpu.make_async_copy(a, b, sems.at[i]) for i, (a, b) in enumerate(zip(hbm, held))]
    for load in loads:
        load.start()
    q_ref, k_ref, v_ref, kt_ref, mine_ref, back_ref, w_vmem = held
    tokens, width = q_ref.shape
    heads = width // DH
    share = tokens // N_HEAD
    for load in loads[:-1]:
        load.wait()

    first_core = lax.rem(lax.axis_index("ctx"), CORES) == 0
    doc = kt_ref[width : width + NOTE, :].astype(f32)[:1]
    mine = jnp.broadcast_to(doc, (DH, tokens)).T
    note = mine_ref[width : width + NOTE, :].astype(f32)
    causal = lax.broadcasted_iota(jnp.int32, (tokens, tokens), 1) <= lax.broadcasted_iota(
        jnp.int32, (tokens, tokens), 0
    )
    wide = jnp.concatenate([mine] * (tokens // DH), axis=1)
    inside = (causal & (wide == doc)).astype(f32)
    prior = (mine == note[0:1]).astype(f32)
    inverse = 1.0 / (
        prior * (16.0 * note[4:5] + note[8:9]) + jnp.sum(inside, axis=1, keepdims=True)
    )
    prior_inverse = prior * inverse
    inside_inverse = inside * jnp.concatenate([inverse] * (tokens // DH), axis=1)

    scales = []
    for h in range(heads):
        cols = slice(h * DH, (h + 1) * DH)
        kt = kt_ref[cols, :]
        ktf = kt.astype(f32)
        mean = jnp.mean(ktf * ktf, axis=0, keepdims=True)
        scale = lax.rsqrt(mean + 1e-06) * (1.0 / math.sqrt(DH))
        scales.append(scale)
        weight[h] = inside_inverse * (scale * scale)
        state = jnp.where(first_core, mine_ref[cols, :], back_ref[cols, :])
        for at in (0, DH):
            right[h, at : at + DH, :tokens] = kt
            right[h, at : at + DH, tokens:] = state
        q = q_ref[:, cols].astype(f32)
        q = q * scale_of(q)
        r_ref[h] = q
        p_ref[h] = q * (1.0 / center)
        x_ref[h] = q * (1.0 / center)

    def products(field, h, times, rows):
        both = dot(split(field), right[h])
        return dot((both[:, :tokens] * times).astype(bf16), rows), both[:, tokens:]

    factor = radius / center
    for _ in range(ITERS):
        factor_new = 1.0 / (2.0 * center / radius - factor)
        for h in range(heads):
            p = p_ref[h]
            within, far = products(p, h, weight[h], k_ref[:, h * DH : (h + 1) * DH])
            r = r_ref[h] - (within + far * prior_inverse + ridge_lambda * p)
            p = (factor_new * factor) * p + (2.0 * factor_new / radius) * r
            r_ref[h] = r
            p_ref[h] = p
            x_ref[h] = x_ref[h] + p
        factor = factor_new

    for h in range(heads):
        cols = slice(h * DH, (h + 1) * DH)
        scale = scales[h]
        state = jnp.where(first_core, back_ref[cols, :], mine_ref[cols, :])
        for at in (0, DH):
            right[h, at : at + DH, tokens:] = state
        within, far = products(x_ref[h], h, inside * scale, v_ref[:, cols])
        o = within + far * prior
        o = o * lax.rsqrt(jnp.mean(o * o, axis=-1, keepdims=True) + 1e-06)
        y_ref[:, cols] = o.astype(bf16)
    me = lax.axis_index("head")
    y = jnp.concatenate(
        [
            y_ref[pl.ds(pl.multiple_of(lax.rem(me + o, N_HEAD) * share, share), share), :]
            for o in OFFSETS
        ],
        axis=0,
    )
    loads[-1].wait()
    model = w_vmem.shape[1]
    tile = 1024
    for c in range(0, model, tile):
        part = dot(y, w_vmem[:, c : c + tile]).astype(bf16)
        for out, (at, lo, hi) in zip(outs, pieces):
            if lo <= c < hi:
                out[:, c - lo : c - lo + tile] = part[at * share : (at + 1) * share]


def solve(pieces, *args):
    tokens, width = args[0].shape
    heads = width // DH
    share = tokens // N_HEAD
    vmem = pl.BlockSpec(memory_space=pltpu.VMEM)
    return pl.pallas_call(
        functools.partial(solve_kernel, pieces),
        out_shape=[jax.ShapeDtypeStruct((share, hi - lo), bf16) for _, lo, hi in pieces],
        in_specs=[pl.BlockSpec(memory_space=pltpu.HBM)] * len(args),
        out_specs=[vmem] * len(pieces),
        scratch_shapes=[
            *[pltpu.VMEM(a.shape, a.dtype) for a in args],
            pltpu.VMEM((heads, 2 * DH, tokens + DH), bf16),
            pltpu.VMEM((heads, tokens, tokens), f32),
            pltpu.VMEM((heads, tokens, DH), f32),
            pltpu.VMEM((heads, tokens, DH), f32),
            pltpu.VMEM((heads, tokens, DH), f32),
            pltpu.VMEM((tokens, width), bf16),
            pltpu.SemaphoreType.DMA((len(args),)),
        ],
        compiler_params=pltpu.CompilerParams(vmem_limit_bytes=LIMIT << 18),
        cost_estimate=pl.CostEstimate(
            flops=12_000_000_000, bytes_accessed=12_000_000, transcendentals=0
        ),
    )(*args)


def prior_states(keep, give):
    rows = keep.shape[0]
    at = rows - NOTE
    size = lax.axis_size("ctx")
    index = lax.axis_index("ctx")
    core = lax.rem(index, CORES)
    x = lax.rem(index // CORES, ROW)
    y = index // (CORES * ROW)
    counted = lax.broadcasted_iota(jnp.int32, (rows, 1), 0)
    counted = (counted < at) | (counted >= at + 4)

    def across(array):
        return lax.ppermute(array, "ctx", [(i, i ^ 1) for i in range(size)])

    def along_x(array, step):
        def target(i):
            c, xx, yy = i % CORES, i // CORES % ROW, i // (CORES * ROW)
            return (yy * ROW + (xx + step) % ROW) * CORES + c

        return lax.ppermute(array, "ctx", [(i, target(i)) for i in range(size)])

    def along_y(array, step):
        return lax.ppermute(
            array, "ctx", [(i, (i + step * CORES * ROW) % size) for i in range(size)]
        )

    def last(array):
        return array[at : at + 1].astype(f32)

    def gated(array, gate):
        return jnp.where(gate & counted, array.astype(f32), 0.0)

    def named(state, document):
        return jnp.where(counted, state, document).astype(bf16)

    other = across(give).astype(f32)
    keep = lax.optimization_barrier(keep.astype(f32))
    early = jnp.where(core == 0, keep, other)
    late = jnp.where(core == 0, other, keep)
    chip = named(
        gated(late, last(late) == last(late)) + gated(early, last(early) == last(late)), last(late)
    )
    one = along_x(chip, 1)
    three = along_x(chip, -1)
    two = along_x(chip, 2)
    row_last = jnp.maximum(
        jnp.maximum(last(one), last(two)), jnp.maximum(last(three), last(chip))
    )
    row = named(
        sum(gated(part, last(part) == row_last) for part in (chip, one, two, three)), row_last
    )
    row_one = along_y(row, 1)
    row_two = along_y(row, 2)
    document = jnp.where(x > 0, last(one), jnp.where(y > 0, last(row_one), -1.0))
    first = sum(
        gated(part, (last(part) == document) & there)
        for part, there in (
            (one, x >= 1),
            (two, x >= 2),
            (three, x >= 3),
            (row_one, y >= 1),
            (row_two, y >= 2),
        )
    )
    second = gated(early, last(early) == last(early)) + jnp.where(
        last(early) == document, first, 0.0
    )
    first = named(first, document)
    second = named(second, last(early))
    mine = jnp.where(core == 0, first, second)
    back = across(jnp.where(core == 0, second, first))
    return mine, back


def shards(queries, keys, values, doc_ids, w_out):
    tokens, width = queries.shape
    model = w_out.shape[1]
    half = model // 2
    doc = doc_ids.reshape(1, tokens)
    vmem = pl.BlockSpec(memory_space=pltpu.VMEM)
    with jax.named_scope("tails"):
        keep, give, kt = pl.pallas_call(
            tails_kernel,
            out_shape=[
                jax.ShapeDtypeStruct((width + NOTE, DH), bf16),
                jax.ShapeDtypeStruct((width + NOTE, DH), bf16),
                jax.ShapeDtypeStruct((width + NOTE, tokens), bf16),
            ],
            in_specs=[vmem] * 3,
            out_specs=[vmem] * 3,
        )(keys, values, doc)
    with jax.named_scope("prior_states"):
        mine, back = prior_states(keep, give)
    pieces = []
    for at in range(N_HEAD):
        pieces += [(at, 0, half), (at, half, model)]
    with jax.named_scope("solve"):
        got = solve(tuple(pieces), queries, keys, values, kt, mine, back, w_out)
    part = {(o, c): got[2 * at + c] for at, o in enumerate(OFFSETS) for c in range(2)}

    size = lax.axis_size("head")

    def hop(array, step):
        return lax.ppermute(array, "head", [(i, (i + step) % size) for i in range(size)])

    def add(*arrays):
        return sum(array.astype(f32) for array in arrays).astype(bf16)

    streams = ((1, 0, 4), (-1, 1, 4), (1, 1, 3), (-1, 0, 3))
    moving = []
    with jax.named_scope("ring"):
        for step, c, hops in streams:
            total = part[hops * step % N_HEAD, c]
            for distance in range(hops - 1, 0, -1):
                total = add(hop(total, step), part[distance * step % N_HEAD, c])
            moving.append(hop(total, step))
    moving = lax.optimization_barrier(tuple(moving))
    columns = [
        add(*[array for array, stream in zip(moving, streams) if stream[1] == c], part[0, c])
        for c in range(2)
    ]
    return jnp.concatenate(columns, axis=1)


def solution(mesh):
    return jax.shard_map(
        shards,
        mesh=mesh,
        in_specs=(P("ctx", "head"), P("ctx", "head"), P("ctx", "head"), P("ctx"), P("head", None)),
        out_specs=P(("ctx", "head"), None),
        check_vma=False,
    )
```

```python
import functools
import math

import jax
import jax.numpy as jnp
from jax import lax
from jax.experimental import pallas as pl
from jax.experimental.pallas import tpu as pltpu
from jax.sharding import PartitionSpec as P

DH = 128
ITERS = 10
N_HEAD = 8
CORES = 2
ROW = 4
COLUMN = 4
NOTE = 16
LIMIT = 198
OFFSETS = (4, 3, 5, 2, 6, 1, 7, 0)

ridge_lambda = 0.02
upper_end = 1.0 + ridge_lambda
center = (upper_end + ridge_lambda) / 2.0
radius = (upper_end - ridge_lambda) / 2.0

f32 = jnp.float32
bf16 = jnp.bfloat16


def dot(a, b):
    return jnp.dot(a, b, preferred_element_type=f32)


def split(field):
    high = field.astype(bf16)
    low = (field - high.astype(f32)).astype(bf16)
    return jnp.concatenate([high, low], axis=1)


def scale_of(rows):
    return lax.rsqrt(jnp.mean(rows * rows, axis=-1, keepdims=True) + 1e-06) * (
        1.0 / math.sqrt(DH)
    )


def tails_kernel(k_ref, v_ref, doc_ref, keep_ref, give_ref, kt_ref):
    tokens, width = k_ref.shape
    heads = width // DH
    doc = doc_ref[...].astype(f32)
    last = jnp.max(doc)
    member_row = (doc == last).astype(f32)
    member = jnp.broadcast_to(member_row, (DH, tokens)).T
    first_core = lax.rem(lax.axis_index("ctx"), CORES) == 0
    for h in range(heads):
        cols = slice(h * DH, (h + 1) * DH)
        k = k_ref[:, cols].astype(f32)
        scale = scale_of(k) * member
        kt = k.T.astype(bf16)
        kt_ref[cols, :] = kt
        right = jnp.concatenate(
            [k * (scale * scale), v_ref[:, cols].astype(f32) * scale], axis=1
        ).astype(bf16)
        state = dot(kt, right)
        key_state, value_state = state[:, :DH], state[:, DH:]
        keep_ref[cols, :] = jnp.where(first_core, key_state, value_state).astype(bf16)
        give_ref[cols, :] = jnp.where(first_core, value_state, key_state).astype(bf16)
    kt_ref[width:, :] = jnp.broadcast_to(doc, (NOTE, tokens)).astype(bf16)
    number = jnp.broadcast_to(jnp.sum(member_row, axis=1, keepdims=True), (8, DH))
    sixteens = jnp.floor(number * (1.0 / 16.0))
    note = jnp.concatenate(
        [jnp.full((4, DH), last), sixteens[:4], number - 16.0 * sixteens], axis=0
    ).astype(bf16)
    keep_ref[width:, :] = note
    give_ref[width:, :] = note


def solve_kernel(pieces, *refs):
    hbm, refs = refs[:7], refs[7:]
    outs, refs = refs[: len(pieces)], refs[len(pieces) :]
    held, (right, weight, p_ref, r_ref, x_ref, y_ref, sems) = refs[:7], refs[7:]
    loads = [pltpu.make_async_copy(a, b, sems.at[i]) for i, (a, b) in enumerate(zip(hbm, held))]
    q_load, k_load, v_load, kt_load, mine_load, back_load, w_load = loads
    for load in (kt_load, mine_load, back_load, q_load, k_load, v_load, w_load):
        load.start()
    q_ref, k_ref, v_ref, kt_ref, mine_ref, back_ref, w_vmem = held
    tokens, width = q_ref.shape
    heads = width // DH
    share = tokens // N_HEAD
    kt_load.wait()
    mine_load.wait()

    first_core = lax.rem(lax.axis_index("ctx"), CORES) == 0
    doc = kt_ref[width : width + NOTE, :].astype(f32)[:1]
    mine = jnp.broadcast_to(doc, (DH, tokens)).T
    note = mine_ref[width : width + NOTE, :].astype(f32)
    causal = lax.broadcasted_iota(jnp.int32, (tokens, tokens), 1) <= lax.broadcasted_iota(
        jnp.int32, (tokens, tokens), 0
    )
    wide = jnp.concatenate([mine] * (tokens // DH), axis=1)
    inside = (causal & (wide == doc)).astype(f32)
    prior = (mine == note[0:1]).astype(f32)
    inverse = 1.0 / (
        prior * (16.0 * note[4:5] + note[8:9]) + jnp.sum(inside, axis=1, keepdims=True)
    )
    prior_inverse = prior * inverse
    inside_inverse = inside * jnp.concatenate([inverse] * (tokens // DH), axis=1)

    back_load.wait()
    q_load.wait()
    scales = []
    for h in range(heads):
        cols = slice(h * DH, (h + 1) * DH)
        kt = kt_ref[cols, :]
        ktf = kt.astype(f32)
        mean = jnp.mean(ktf * ktf, axis=0, keepdims=True)
        scale = lax.rsqrt(mean + 1e-06) * (1.0 / math.sqrt(DH))
        scales.append(scale)
        weight[h] = inside_inverse * (scale * scale)
        state = jnp.where(first_core, mine_ref[cols, :], back_ref[cols, :])
        for at in (0, DH):
            right[h, at : at + DH, :tokens] = kt
            right[h, at : at + DH, tokens:] = state
        q = q_ref[:, cols].astype(f32)
        q = q * scale_of(q)
        r_ref[h] = q
        p_ref[h] = q * (1.0 / center)
        x_ref[h] = q * (1.0 / center)

    def products(field, h, times, rows):
        both = dot(split(field), right[h])
        return dot((both[:, :tokens] * times).astype(bf16), rows), both[:, tokens:]

    k_load.wait()
    factor = radius / center
    for _ in range(ITERS):
        factor_new = 1.0 / (2.0 * center / radius - factor)
        for h in range(heads):
            p = p_ref[h]
            within, far = products(p, h, weight[h], k_ref[:, h * DH : (h + 1) * DH])
            r = r_ref[h] - (within + far * prior_inverse + ridge_lambda * p)
            p = (factor_new * factor) * p + (2.0 * factor_new / radius) * r
            r_ref[h] = r
            p_ref[h] = p
            x_ref[h] = x_ref[h] + p
        factor = factor_new

    v_load.wait()
    for h in range(heads):
        cols = slice(h * DH, (h + 1) * DH)
        scale = scales[h]
        state = jnp.where(first_core, back_ref[cols, :], mine_ref[cols, :])
        for at in (0, DH):
            right[h, at : at + DH, tokens:] = state
        within, far = products(x_ref[h], h, inside * scale, v_ref[:, cols])
        o = within + far * prior
        o = o * lax.rsqrt(jnp.mean(o * o, axis=-1, keepdims=True) + 1e-06)
        y_ref[:, cols] = o.astype(bf16)
    me = lax.axis_index("head")
    y = jnp.concatenate(
        [
            y_ref[pl.ds(pl.multiple_of(lax.rem(me + o, N_HEAD) * share, share), share), :]
            for o in OFFSETS
        ],
        axis=0,
    )
    w_load.wait()
    model = w_vmem.shape[1]
    tile = 1024
    for c in range(0, model, tile):
        part = dot(y, w_vmem[:, c : c + tile]).astype(bf16)
        for out, (at, lo, hi) in zip(outs, pieces):
            if lo <= c < hi:
                out[:, c - lo : c - lo + tile] = part[at * share : (at + 1) * share]


def solve(pieces, *args):
    tokens, width = args[0].shape
    heads = width // DH
    share = tokens // N_HEAD
    vmem = pl.BlockSpec(memory_space=pltpu.VMEM)
    return pl.pallas_call(
        functools.partial(solve_kernel, pieces),
        out_shape=[jax.ShapeDtypeStruct((share, hi - lo), bf16) for _, lo, hi in pieces],
        in_specs=[pl.BlockSpec(memory_space=pltpu.HBM)] * len(args),
        out_specs=[vmem] * len(pieces),
        scratch_shapes=[
            *[pltpu.VMEM(a.shape, a.dtype) for a in args],
            pltpu.VMEM((heads, 2 * DH, tokens + DH), bf16),
            pltpu.VMEM((heads, tokens, tokens), f32),
            pltpu.VMEM((heads, tokens, DH), f32),
            pltpu.VMEM((heads, tokens, DH), f32),
            pltpu.VMEM((heads, tokens, DH), f32),
            pltpu.VMEM((tokens, width), bf16),
            pltpu.SemaphoreType.DMA((len(args),)),
        ],
        compiler_params=pltpu.CompilerParams(vmem_limit_bytes=LIMIT << 18),
        cost_estimate=pl.CostEstimate(
            flops=12_000_000_000, bytes_accessed=12_000_000, transcendentals=0
        ),
    )(*args)


def prior_states(keep, give):
    rows = keep.shape[0]
    at = rows - NOTE
    size = lax.axis_size("ctx")
    index = lax.axis_index("ctx")
    core = lax.rem(index, CORES)
    x = lax.rem(index // CORES, ROW)
    y = index // (CORES * ROW)
    counted = lax.broadcasted_iota(jnp.int32, (rows, 1), 0)
    counted = (counted < at) | (counted >= at + 4)

    def across(array):
        return lax.ppermute(array, "ctx", [(i, i ^ 1) for i in range(size)])

    def along_x(array, step):
        def target(i):
            c, xx, yy = i % CORES, i // CORES % ROW, i // (CORES * ROW)
            return (yy * ROW + (xx + step) % ROW) * CORES + c

        return lax.ppermute(array, "ctx", [(i, target(i)) for i in range(size)])

    def along_y(array, step):
        return lax.ppermute(
            array, "ctx", [(i, (i + step * CORES * ROW) % size) for i in range(size)]
        )

    def last(array):
        return array[at : at + 1].astype(f32)

    def gated(array, gate):
        return jnp.where(gate & counted, array.astype(f32), 0.0)

    def named(state, document):
        return jnp.where(counted, state, document).astype(bf16)

    other = across(give).astype(f32)
    keep = lax.optimization_barrier(keep.astype(f32))
    early = jnp.where(core == 0, keep, other)
    late = jnp.where(core == 0, other, keep)
    chip = named(
        gated(late, last(late) == last(late)) + gated(early, last(early) == last(late)), last(late)
    )
    one = along_x(chip, 1)
    three = along_x(chip, -1)
    two = along_x(chip, 2)
    row_last = jnp.maximum(
        jnp.maximum(last(one), last(two)), jnp.maximum(last(three), last(chip))
    )
    row = named(
        sum(gated(part, last(part) == row_last) for part in (chip, one, two, three)), row_last
    )
    row_one = along_y(row, 1)
    row_two = along_y(row, 2)
    document = jnp.where(x > 0, last(one), jnp.where(y > 0, last(row_one), -1.0))
    first = sum(
        gated(part, (last(part) == document) & there)
        for part, there in (
            (one, x >= 1),
            (two, x >= 2),
            (three, x >= 3),
            (row_one, y >= 1),
            (row_two, y >= 2),
        )
    )
    second = gated(early, last(early) == last(early)) + jnp.where(
        last(early) == document, first, 0.0
    )
    first = named(first, document)
    second = named(second, last(early))
    mine = jnp.where(core == 0, first, second)
    back = across(jnp.where(core == 0, second, first))
    return mine, back


def shards(queries, keys, values, doc_ids, w_out):
    tokens, width = queries.shape
    model = w_out.shape[1]
    half = model // 2
    doc = doc_ids.reshape(1, tokens)
    vmem = pl.BlockSpec(memory_space=pltpu.VMEM)
    with jax.named_scope("tails"):
        keep, give, kt = pl.pallas_call(
            tails_kernel,
            out_shape=[
                jax.ShapeDtypeStruct((width + NOTE, DH), bf16),
                jax.ShapeDtypeStruct((width + NOTE, DH), bf16),
                jax.ShapeDtypeStruct((width + NOTE, tokens), bf16),
            ],
            in_specs=[vmem] * 3,
            out_specs=[vmem] * 3,
        )(keys, values, doc)
    with jax.named_scope("prior_states"):
        mine, back = prior_states(keep, give)
    pieces = []
    for at in range(N_HEAD):
        pieces += [(at, 0, half), (at, half, model)]
    with jax.named_scope("solve"):
        got = solve(tuple(pieces), queries, keys, values, kt, mine, back, w_out)
    part = {(o, c): got[2 * at + c] for at, o in enumerate(OFFSETS) for c in range(2)}

    size = lax.axis_size("head")

    def hop(array, step):
        return lax.ppermute(array, "head", [(i, (i + step) % size) for i in range(size)])

    def add(*arrays):
        return sum(array.astype(f32) for array in arrays).astype(bf16)

    streams = ((1, 0, 4), (-1, 1, 4), (1, 1, 3), (-1, 0, 3))
    moving = []
    with jax.named_scope("ring"):
        for step, c, hops in streams:
            total = part[hops * step % N_HEAD, c]
            for distance in range(hops - 1, 0, -1):
                total = add(hop(total, step), part[distance * step % N_HEAD, c])
            moving.append(hop(total, step))
    moving = lax.optimization_barrier(tuple(moving))
    columns = [
        add(*[array for array, stream in zip(moving, streams) if stream[1] == c], part[0, c])
        for c in range(2)
    ]
    return jnp.concatenate(columns, axis=1)


def solution(mesh):
    return jax.shard_map(
        shards,
        mesh=mesh,
        in_specs=(P("ctx", "head"), P("ctx", "head"), P("ctx", "head"), P("ctx"), P("head", None)),
        out_specs=P(("ctx", "head"), None),
        check_vma=False,
    )
```
